32 devices in a mesh: groups: 2 (over y), row: 8 (over z, x), col: 2 (over core).
Axes of the slice: x: 2, y: 2, z: 4, core: 2. Of those that a mesh axis runs over, the one named last changes fastest.
Arguments:
- tokens: bfloat16 [1024, 4096], P(('groups', 'row'), 'col'), parts along dimension 0, may hold values from -6 to 6
- up_weight: bfloat16 [4096, 32768], P('col', 'row'), may hold values from -0.09375 to 0.09375
- down_weight: bfloat16 [32768, 4096], P('row', 'col'), may hold values from -0.03125 to 0.03125
- cotangent: bfloat16 [1024, 4096], P(('groups', 'row'), 'col'), parts along dimension 0, may hold values from -6 to 6
Outputs:
- grad_input: bfloat16 [1024, 4096], P(('groups', 'row'), 'col'), parts along dimension 0
- grad_up: bfloat16 [8192, 32768], P(('groups', 'col'), 'row'), parts along dimension 0
- grad_down: bfloat16 [65536, 4096], P(('groups', 'row'), 'col'), parts along dimension 0
The draws below stay inside these ranges and needn't reach their ends.
There are 2 independent parts, one for each index of `groups`. The reference program is written for one: setup_inputs(seed, part) draws one part's arguments, and reference() takes and returns one part's arrays. A program takes and returns all parts, laid end to end along the dimension named above; an argument that names none is the same for every part. Nothing has to cross between parts.
All inputs are finite; a program needn't handle non-finite values.
Results may differ from the reference program's by a relative error of at most 0.0051.
Values may be sent and summed in bfloat16 or wider, within the bound.
No kernel may reach another device: no remote copies, remote signals or barrier semaphores. Data moves between devices by JAX's collectives and lax.ppermute only.
A program may use at most 192 MiB of HBM per device.

```python
import jax
import jax.numpy as jnp
from jax import lax

D = 4096
FF_WIN = 32768
TOKENS = 512


def levels(own_key, shape, pieces, low, high):
    gain = 1.0
    for axis_at, shards_of in pieces:
        draws = jax.random.uniform(jax.random.fold_in(jax.random.fold_in(own_key, 6), axis_at), (shards_of,), jnp.float32, low / len(pieces), high / len(pieces))
        gain = gain * jnp.repeat(jnp.exp(draws), shape[axis_at] // shards_of).reshape((-1,) + (1,) * (len(shape) - 1 - axis_at))
    return gain


def noise(stream_key, extent, deviation, bound, cuts=(), held_as=jnp.bfloat16):
    values = deviation * jax.random.normal(stream_key, extent, jnp.float32)
    if cuts:
        values = values * levels(stream_key, extent, cuts, -0.22, 0.18)
    return jnp.clip(values, -bound, bound).astype(held_as)


def setup_inputs(seed: int = 0, part: int = 0) -> dict:
    splits = jax.random.split(jax.random.key(seed), 5)
    own_keys = jax.random.split(jax.random.fold_in(splits[4], part), 5)
    return {
        "tokens": noise(own_keys[0], (TOKENS, D), 1.0, 6.0, ((0, 8), (1, 2))),
        "up_weight": noise(splits[1], (D, FF_WIN), D ** -0.5, 0.09375, ((0, 2), (1, 8))),
        "down_weight": noise(splits[2], (FF_WIN, D), FF_WIN ** -0.5, 0.03125, ((0, 8), (1, 2))),
        "cotangent": noise(own_keys[3], (TOKENS, D), 1.0, 6.0, ((0, 8), (1, 2))),
    }


def gelu_parts(preact):
    argument = 0.7978845608 * (preact + 0.044715 * preact * preact * preact)
    curve_term = jnp.tanh(argument)
    activated = 0.5 * preact * (1.0 + curve_term)
    factor = 0.5 * (1.0 + curve_term) + 0.5 * preact * (1.0 - curve_term * curve_term) * 0.7978845608 * (1.0 + 3.0 * 0.044715 * preact * preact)
    return activated, factor


def reference(tokens, up_weight, down_weight, cotangent):
    preact = jnp.dot(tokens, up_weight, preferred_element_type=jnp.float32)
    back_grad = lax.dot_general(cotangent, down_weight, (((1,), (1,)), ((), ())), preferred_element_type=jnp.float32)
    activated, factor = gelu_parts(preact)
    activated = activated.astype(jnp.bfloat16)
    delta = (back_grad * factor).astype(jnp.bfloat16)
    grad_down = lax.dot_general(activated, cotangent, (((0,), (0,)), ((), ())), preferred_element_type=jnp.float32)
    grad_up = lax.dot_general(tokens, delta, (((0,), (0,)), ((), ())), preferred_element_type=jnp.float32)
    grad_input = lax.dot_general(delta, up_weight, (((1,), (1,)), ((), ())), preferred_element_type=jnp.float32)
    return grad_input.astype(jnp.bfloat16), grad_up.astype(jnp.bfloat16), grad_down.astype(jnp.bfloat16)
```

```python
import functools

import jax
import jax.numpy as jnp
from jax import lax
from jax.experimental import pallas as pl
from jax.experimental.pallas import tpu as pltpu
from jax.sharding import PartitionSpec as P

F32 = jnp.float32
BF16 = jnp.bfloat16
VMEM_LIMIT = 56 * 1024 * 1024
NX = 2
NT = (((1,), (1,)), ((), ()))
TN = (((0,), (0,)), ((), ()))


def gelu_parts(preact):
    argument = 0.7978845608 * (preact + 0.044715 * preact * preact * preact)
    curve_term = jnp.tanh(argument)
    activated = 0.5 * preact * (1.0 + curve_term)
    factor = 0.5 * (1.0 + curve_term) + 0.5 * preact * (
        1.0 - curve_term * curve_term
    ) * 0.7978845608 * (1.0 + 3.0 * 0.044715 * preact * preact)
    return (activated, factor)


def params():
    return pltpu.CompilerParams(vmem_limit_bytes=VMEM_LIMIT)


def cost(flops, moved, transcendentals=0):
    return pl.CostEstimate(
        flops=flops, bytes_accessed=moved, transcendentals=transcendentals
    )


def stacked(refs, which):
    return jnp.concatenate([r[which] for r in refs], axis=0)


def hidden_pass(core, own, other, up, up_other, down, down_other):
    n = len(own)
    rows, feats = own[0].shape[1:]
    m = n * rows
    half = up_other.shape[1]
    tile = min(512, half)
    steps = half // tile

    def kernel(core_ref, *refs):
        own_refs, other_refs = refs[:n], refs[n : 2 * n]
        up_ref, up2_ref, down_ref, down2_ref, act_ref, delta_ref = refs[2 * n :]
        tok, tok2 = stacked(own_refs, 0), stacked(other_refs, 0)
        cot, cot2 = stacked(own_refs, 1), stacked(other_refs, 1)
        preact = jnp.dot(tok, up_ref[...], preferred_element_type=F32) + jnp.dot(
            tok2, up2_ref[...], preferred_element_type=F32
        )
        back = lax.dot_general(
            cot, down_ref[...], NT, preferred_element_type=F32
        ) + lax.dot_general(cot2, down2_ref[...], NT, preferred_element_type=F32)
        activated, factor = gelu_parts(preact)
        act_ref[...] = activated.astype(BF16)
        delta_ref[...] = (back * factor).astype(BF16)

    piece = pl.BlockSpec((2, rows, feats), lambda i, c: (0, 0, 0))
    out = pl.BlockSpec((m, tile), lambda i, c: (0, i))
    return pl.pallas_call(
        kernel,
        grid_spec=pltpu.PrefetchScalarGridSpec(
            num_scalar_prefetch=1,
            grid=(steps,),
            in_specs=[piece] * (2 * n)
            + [
                pl.BlockSpec((feats, tile), lambda i, c: (0, c[0] * steps + i)),
                pl.BlockSpec((feats, tile), lambda i, c: (0, i)),
                pl.BlockSpec((tile, feats), lambda i, c: (c[0] * steps + i, 0)),
                pl.BlockSpec((tile, feats), lambda i, c: (i, 0)),
            ],
            out_specs=[out, out],
        ),
        out_shape=[jax.ShapeDtypeStruct((m, half), BF16)] * 2,
        compiler_params=params(),
        cost_estimate=cost(
            8 * m * feats * half, 8 * half * feats + 16 * m * feats, m * half
        ),
    )(core, *own, *other, up, up_other, down, down_other)


def input_pass(core, delta, delta_other, up, first, count):
    m, half = delta.shape
    tile = min(512, count)
    steps = count // tile
    base = first // tile
    keep = m // NX

    def kernel(core_ref, d_ref, d2_ref, up_ref, up2_ref, keep_ref, send_ref):
        total = lax.dot_general(
            d_ref[...], up_ref[...], NT, preferred_element_type=F32
        ) + lax.dot_general(d2_ref[...], up2_ref[...], NT, preferred_element_type=F32)
        keep_ref[...] = total[:keep]
        send_ref[...] = total[keep:].astype(BF16)

    rows = pl.BlockSpec((m, half), lambda i, c: (0, 0))
    return pl.pallas_call(
        kernel,
        grid_spec=pltpu.PrefetchScalarGridSpec(
            num_scalar_prefetch=1,
            grid=(steps,),
            in_specs=[
                rows,
                rows,
                pl.BlockSpec((tile, half), lambda i, c: (base + i, c[0])),
                pl.BlockSpec((tile, half), lambda i, c: (base + i, 1 - c[0])),
            ],
            out_specs=[
                pl.BlockSpec((keep, tile), lambda i, c: (0, i)),
                pl.BlockSpec((m - keep, tile), lambda i, c: (0, i)),
            ],
        ),
        out_shape=[
            jax.ShapeDtypeStruct((keep, count), F32),
            jax.ShapeDtypeStruct((m - keep, count), BF16),
        ],
        compiler_params=params(),
        cost_estimate=cost(4 * m * half * count, 4 * count * half + 4 * m * half),
    )(core, delta, delta_other, up, up)


def down_pass(core, acts, pieces, hidden, flip, into=None):
    parts, n = len(acts), len(pieces)
    m, half = acts[0].shape
    rows, feats = pieces[0].shape[1:]
    tile = min(512, half)
    steps = half // tile

    def kernel(core_ref, *refs):
        act = jnp.concatenate([r[...] for r in refs[:parts]], axis=0)
        cot = stacked(refs[parts : parts + n], 0)
        refs[-1][...] = lax.dot_general(
            act, cot, TN, preferred_element_type=F32
        ).astype(BF16)

    extra = [] if into is None else [into]

    def place(i, c):
        side = 1 - c[0] if flip else c[0]
        return (side * steps + i, 0)

    return pl.pallas_call(
        kernel,
        grid_spec=pltpu.PrefetchScalarGridSpec(
            num_scalar_prefetch=1,
            grid=(steps,),
            in_specs=[pl.BlockSpec((m, tile), lambda i, c: (0, i))] * parts
            + [pl.BlockSpec((1, rows, feats), lambda i, c: (1, 0, 0))] * n
            + [pl.BlockSpec(memory_space=pl.ANY)] * len(extra),
            out_specs=pl.BlockSpec((tile, feats), place),
        ),
        out_shape=jax.ShapeDtypeStruct((hidden, feats), BF16),
        input_output_aliases={1 + parts + n: 0} if extra else {},
        compiler_params=params(),
        cost_estimate=cost(
            2 * parts * m * half * feats, 2 * half * feats + 2 * parts * m * (half + feats)
        ),
    )(core, *acts, *pieces, *extra)


def up_pass(core, deltas, deltas_other, pieces, hidden):
    parts, n = len(deltas), len(pieces)
    m, half = deltas[0].shape
    rows, feats = pieces[0].shape[1:]
    tile = min(512, half)
    steps = half // tile

    def kernel(core_ref, *refs):
        tok = stacked(refs[2 * parts : 2 * parts + n], 0)

        def emit(these):
            delta = jnp.concatenate([r[...] for r in these], axis=0)
            refs[-1][...] = lax.dot_general(
                tok, delta, TN, preferred_element_type=F32
            ).astype(BF16)

        @pl.when(pl.program_id(0) < steps)
        def _():
            emit(refs[:parts])

        @pl.when(pl.program_id(0) >= steps)
        def _():
            emit(refs[parts : 2 * parts])

    def place(i, c):
        side = jnp.where(i < steps, c[0], 1 - c[0])
        return (0, side * steps + i % steps)

    return pl.pallas_call(
        kernel,
        grid_spec=pltpu.PrefetchScalarGridSpec(
            num_scalar_prefetch=1,
            grid=(2 * steps,),
            in_specs=[
                pl.BlockSpec((m, tile), lambda i, c: (0, jnp.minimum(i, steps - 1)))
            ]
            * parts
            + [pl.BlockSpec((m, tile), lambda i, c: (0, jnp.maximum(i - steps, 0)))]
            * parts
            + [pl.BlockSpec((1, rows, feats), lambda i, c: (0, 0, 0))] * n,
            out_specs=pl.BlockSpec((feats, tile), place),
        ),
        out_shape=jax.ShapeDtypeStruct((feats, hidden), BF16),
        compiler_params=params(),
        cost_estimate=cost(
            4 * parts * m * half * feats,
            4 * half * feats + 2 * parts * m * (2 * half + feats),
        ),
    )(core, *deltas, *deltas_other, *pieces)


def split_plan(row, tokens, up_weight, down_weight, cotangent):
    nz = row // NX
    mine, feats = tokens.shape
    hidden = up_weight.shape[1]
    half = hidden // 2
    core_at = lax.axis_index("col")
    core = core_at.astype(jnp.int32)[None]

    def swap(x):
        return lax.ppermute(x, "col", [(0, 1), (1, 0)])

    def across(x):
        return lax.ppermute(x, "row", [(r, r ^ 1) for r in range(row)])

    def shift(x, k):
        return lax.ppermute(
            x, "row", [(r, (r + k * NX) % row) for r in range(row)]
        )

    own_piece = jnp.stack([tokens, cotangent])
    order = [0] + [k for j in range(1, nz // 2 + 1) for k in sorted({j, nz - j})]
    chunks = [order[: nz // 2], order[nz // 2 :]]
    same = {k: own_piece if k == 0 else shift(own_piece, k) for k in order}
    facing = {k: across(same[k]) for k in order}

    other_half = (1 - core_at) * half
    up_other = swap(lax.dynamic_slice(up_weight, (0, other_half), (feats, half)))
    down_other = swap(lax.dynamic_slice(down_weight, (other_half, 0), (half, feats)))

    all_pieces, acts, acts2, deltas, deltas2 = [], [], [], [], []
    for ks in chunks:
        pieces = [same[k] for k in ks] + [facing[k] for k in ks]
        all_pieces += pieces
        act, delta = hidden_pass(
            core,
            pieces,
            [swap(p) for p in pieces],
            up_weight,
            up_other,
            down_weight,
            down_other,
        )
        deltas.append(delta)
        acts.append(act)
        deltas2.append(swap(delta))
        acts2.append(swap(act))

    grad_down = down_pass(core, acts, all_pieces, hidden, False)

    splits = 2
    width = feats // splits
    columns = [[None, []] for _ in range(splits)]
    for ks, delta, delta2 in zip(chunks, deltas, deltas2):
        for s in range(splits):
            kept, sent = input_pass(core, delta, delta2, up_weight, s * width, width)
            total = kept + across(sent).astype(F32)
            for at, k in enumerate(ks):
                block = total[at * mine : (at + 1) * mine]
                if k == 0:
                    columns[s][0] = block
                else:
                    columns[s][1].append(shift(block.astype(BF16), -k))

    grad_up = up_pass(core, deltas, deltas2, all_pieces, hidden)
    grad_down = down_pass(core, acts2, all_pieces, hidden, True, grad_down)
    done = []
    for first, rest in columns:
        for block in rest:
            first = first + block.astype(F32)
        done.append(first.astype(BF16))
    return (jnp.concatenate(done, axis=1), grad_up, grad_down)


def whole_plan(tokens, up_weight, down_weight, cotangent):
    gathered = functools.partial(lax.all_gather, axis_name="row", axis=0, tiled=True)
    panel_tokens, panel_cotangent = gathered(tokens), gathered(cotangent)
    pre_part = jnp.dot(panel_tokens, up_weight, preferred_element_type=F32)
    back_part = lax.dot_general(
        panel_cotangent, down_weight, NT, preferred_element_type=F32
    )
    preact, back_grad = lax.psum((pre_part, back_part), "col")
    activated, factor = gelu_parts(preact)
    activated = activated.astype(BF16)
    delta = (back_grad * factor).astype(BF16)
    grad_down = lax.dot_general(
        activated, panel_cotangent, TN, preferred_element_type=F32
    )
    grad_up = lax.dot_general(panel_tokens, delta, TN, preferred_element_type=F32)
    grad_input = lax.psum_scatter(
        lax.dot_general(delta, up_weight, NT, preferred_element_type=F32),
        "row",
        scatter_dimension=0,
        tiled=True,
    )
    return (grad_input.astype(BF16), grad_up.astype(BF16), grad_down.astype(BF16))


def solution(mesh):
    row, col = mesh.shape["row"], mesh.shape["col"]

    def per_device(tokens, up_weight, down_weight, cotangent):
        args = (tokens, up_weight, down_weight, cotangent)
        short = row == 8 and tokens.shape[0] % 16 == 0
        if col == 2 and short:
            return split_plan(row, *args)
        return whole_plan(*args)

    in_specs = (
        P(("groups", "row"), "col"),
        P("col", "row"),
        P("row", "col"),
        P(("groups", "row"), "col"),
    )
    out_specs = (
        P(("groups", "row"), "col"),
        P(("groups", "col"), "row"),
        P(("groups", "row"), "col"),
    )
    return jax.shard_map(
        per_device, mesh=mesh, in_specs=in_specs, out_specs=out_specs, check_vma=False
    )
```

```python
import functools

import jax
import jax.numpy as jnp
from jax import lax
from jax.experimental import pallas as pl
from jax.experimental.pallas import tpu as pltpu
from jax.sharding import PartitionSpec as P

F32 = jnp.float32
BF16 = jnp.bfloat16
VMEM_LIMIT = 36 * 1024 * 1024
NX = 2
PARTS = 2
SPLITS = 2
Z_AHEAD = 3
X_AHEAD = 2
PRE_TILE = 1024
BACK_TILE = 1024
IN_TILE = 256
NT = (((1,), (1,)), ((), ()))
TN = (((0,), (0,)), ((), ()))


def gelu_parts(preact):
    square = preact * preact
    curve_term = jnp.tanh(preact * (0.7978845608 + (0.7978845608 * 0.044715) * square))
    gate = 0.5 + 0.5 * curve_term
    slope = 0.5 * 0.7978845608 + (1.5 * 0.044715 * 0.7978845608) * square
    factor = gate + preact * (1.0 - curve_term * curve_term) * slope
    return (preact * gate, factor)


def params():
    return pltpu.CompilerParams(vmem_limit_bytes=VMEM_LIMIT)


def cost(flops, moved, transcendentals=0):
    return pl.CostEstimate(
        flops=flops // 20, bytes_accessed=moved // 20, transcendentals=0
    )


def joined(refs):
    return jnp.concatenate([r[...] for r in refs], axis=0)


def call(kernel, steps, in_specs, out_specs, out_shape, estimate, args, scratch=()):
    return pl.pallas_call(
        kernel,
        grid=(steps,),
        in_specs=in_specs,
        out_specs=out_specs,
        out_shape=out_shape,
        scratch_shapes=list(scratch),
        compiler_params=params(),
        cost_estimate=estimate,
    )(*args)


def whole(x):
    return pl.BlockSpec(x.shape, lambda i: (0, 0))


def pre_pass(tokens, up, first, hidden):
    n = len(tokens)
    rows, feats = tokens[0].shape
    m = n * rows
    tile = min(PRE_TILE, hidden)
    base = first // tile

    def kernel(*refs):
        up_ref, out_ref = refs[n:]
        out_ref[...] = jnp.dot(
            joined(refs[:n]), up_ref[...], preferred_element_type=F32
        ).astype(BF16)

    return call(
        kernel,
        hidden // tile,
        [whole(t) for t in tokens]
        + [pl.BlockSpec((feats, tile), lambda i: (0, base + i))],
        pl.BlockSpec((m, tile), lambda i: (0, i)),
        jax.ShapeDtypeStruct((m, hidden), BF16),
        cost(2 * m * feats * hidden, 2 * feats * hidden + m * (2 * feats + 2 * hidden)),
        (*tokens, up),
    )


def back_pass(cots, down, pre, pre_other, first):
    n = len(cots)
    rows, feats = cots[0].shape
    m, hidden = pre.shape
    tile = min(BACK_TILE, hidden)
    base = first // tile

    def kernel(*refs):
        down_ref, pre_ref, pre2_ref, act_ref, delta_ref = refs[n:]
        back = lax.dot_general(
            joined(refs[:n]), down_ref[...], NT, preferred_element_type=F32
        )
        activated, factor = gelu_parts(
            pre_ref[...].astype(F32) + pre2_ref[...].astype(F32)
        )
        act_ref[...] = activated.astype(BF16)
        delta_ref[...] = (back * factor).astype(BF16)

    column = pl.BlockSpec((m, tile), lambda i: (0, i))
    return call(
        kernel,
        hidden // tile,
        [whole(c) for c in cots]
        + [pl.BlockSpec((tile, feats), lambda i: (base + i, 0)), column, column],
        [column, column],
        [jax.ShapeDtypeStruct((m, hidden), BF16)] * 2,
        cost(
            2 * m * feats * hidden,
            2 * feats * hidden + m * (2 * feats + 8 * hidden),
            m * hidden,
        ),
        (*cots, down, pre, pre_other),
    )


def summed(left, right):
    return (left.astype(F32) + right.astype(F32)).astype(BF16)


def input_pass(deltas, up, first, count):
    parts = len(deltas) // 2
    m, each = deltas[0].shape
    hidden = max(parts, 1) * each
    tile = min(IN_TILE, count)
    base = first // tile
    keep = m // NX

    def kernel(*refs):
        up_ref, keep_ref, send_ref = refs[len(deltas) : len(deltas) + 3]
        if parts:
            total_ref = refs[-1]

            @pl.when(pl.program_id(0) == 0)
            def _():
                for p in range(parts):
                    total_ref[:, p * each : (p + 1) * each] = summed(
                        refs[p][...], refs[parts + p][...]
                    )

        else:
            total_ref = refs[0]
        out = lax.dot_general(
            total_ref[...], up_ref[...], NT, preferred_element_type=F32
        )
        keep_ref[...] = out[:keep]
        send_ref[...] = out[keep:].astype(BF16)

    out_specs = [
        pl.BlockSpec((keep, tile), lambda i: (0, i)),
        pl.BlockSpec((m - keep, tile), lambda i: (0, i)),
    ]
    out_shape = [
        jax.ShapeDtypeStruct((keep, count), F32),
        jax.ShapeDtypeStruct((m - keep, count), BF16),
    ]
    if parts:
        out_specs.append(pl.BlockSpec((m, hidden), lambda i: (0, 0)))
        out_shape.append(jax.ShapeDtypeStruct((m, hidden), BF16))
    got = call(
        kernel,
        count // tile,
        [whole(d) for d in deltas]
        + [pl.BlockSpec((tile, hidden), lambda i: (base + i, 0))],
        out_specs,
        out_shape,
        cost(2 * m * hidden * count, 2 * count * hidden + 4 * m * hidden),
        (*deltas, up),
    )
    return got if parts else (*got, deltas[0])


def down_pass(act, cots, part, parts, into=None):
    n = len(cots)
    m, each = act.shape
    rows, feats = cots[0].shape
    tile = min(512, each)
    steps = each // tile
    extra = [] if into is None else [into]

    def kernel(*refs):
        refs[-1][...] = lax.dot_general(
            refs[0][...], joined(refs[1 : 1 + n]), TN, preferred_element_type=F32
        ).astype(BF16)

    return pl.pallas_call(
        kernel,
        grid=(steps,),
        in_specs=[pl.BlockSpec((m, tile), lambda i: (0, i))]
        + [whole(c) for c in cots]
        + [pl.BlockSpec(memory_space=pl.ANY)] * len(extra),
        out_specs=pl.BlockSpec((tile, feats), lambda i: (part * steps + i, 0)),
        out_shape=jax.ShapeDtypeStruct((parts * each, feats), BF16),
        input_output_aliases={1 + n: 0} if extra else {},
        compiler_params=params(),
        cost_estimate=cost(
            2 * m * each * feats, 2 * each * feats + 2 * m * (each + feats)
        ),
    )(act, *cots, *extra)


def up_pass(delta, tokens, part, parts, into=None):
    n = len(tokens)
    m, hidden = delta.shape
    rows, feats = tokens[0].shape
    each = hidden // parts
    tile = min(512, each)
    steps = each // tile
    extra = [] if into is None else [into]

    def kernel(*refs):
        refs[-1][...] = lax.dot_general(
            joined(refs[1 : 1 + n]), refs[0][...], TN, preferred_element_type=F32
        ).astype(BF16)

    return pl.pallas_call(
        kernel,
        grid=(steps,),
        in_specs=[pl.BlockSpec((m, tile), lambda i: (0, part * steps + i))]
        + [whole(t) for t in tokens]
        + [pl.BlockSpec(memory_space=pl.ANY)] * len(extra),
        out_specs=pl.BlockSpec((feats, tile), lambda i: (0, part * steps + i)),
        out_shape=jax.ShapeDtypeStruct((feats, hidden), BF16),
        input_output_aliases={1 + n: 0} if extra else {},
        compiler_params=params(),
        cost_estimate=cost(
            2 * m * each * feats, 2 * each * feats + 2 * m * (each + feats)
        ),
    )(delta, *tokens, *extra)


def tied(x, *after):
    return lax.optimization_barrier((x,) + after)[0] if after else x


def split_plan(row, tokens, up_weight, down_weight, cotangent):
    nz = row // NX
    mine, feats = tokens.shape

    def swap(x):
        return lax.ppermute(x, "col", [(0, 1), (1, 0)])

    def across(x):
        return lax.ppermute(x, "row", [(r, r ^ 1) for r in range(row)])

    def shift(x, k):
        return lax.ppermute(x, "row", [(r, (r + k * NX) % row) for r in range(row)])

    order = [0] + [k for j in range(1, nz // 2 + 1) for k in sorted({j, nz - j})]
    near, far = order[1:-1], order[-1]
    same = {("t", 0): tokens, ("c", 0): cotangent}
    facing, sent, crossed = {}, [], []
    for name, block, ks in (
        ("t", tokens, near + [far]),
        ("c", cotangent, near + [far]),
    ):
        for k in ks:
            tie = sent[-Z_AHEAD:][:1] if len(sent) >= Z_AHEAD else ()
            same[name, k] = shift(tied(block, *tie), k)
            sent.append(same[name, k])
    queue = [("t", 0), ("t", near[0]), ("c", 0)]
    queue += [("t", k) for k in near[1:] + [far]]
    queue += [("c", k) for k in near + [far]]
    for at in queue:
        tie = crossed[-X_AHEAD:][:1] if len(crossed) >= X_AHEAD else ()
        facing[at] = across(tied(same[at], *tie))
        crossed.append(facing[at])

    def pieces(name):
        return [same[name, k] for k in order] + [facing[name, k] for k in order]

    def after(blocks, *events):
        return [tied(blocks[0], *events)] + list(blocks[1:])

    hidden = up_weight.shape[1]
    each = hidden // 2
    all_tokens, all_cots = pieces("t"), pieces("c")
    pre0 = pre_pass(all_tokens, up_weight, 0, each)
    events = [pre0] + sent[len(near) + 1 :] + crossed[-1 - len(near) : -1]
    pre1 = pre_pass(after(all_tokens, *events), up_weight, each, each)
    other0, other1 = swap(pre0), swap(pre1)
    act0, delta0 = back_pass(after(all_cots, pre1), down_weight, pre0, other0, 0)
    act1, delta1 = back_pass(after(all_cots, delta0), down_weight, pre1, other1, each)
    deltas = [delta0, delta1, swap(delta0), swap(delta1)]
    grad_down = down_pass(tied(act0, delta1), all_cots, 0, 2)

    width = feats // SPLITS
    kepts, gones = [], []
    last = grad_down
    for s in range(SPLITS):
        kept, gone, delta = input_pass(
            after(deltas, last), up_weight, s * width, width
        )
        deltas, last = [delta], kept
        kepts.append(kept)
        gones.append(across(gone))
    grad_down = down_pass(tied(act1, last), all_cots, 1, 2, grad_down)
    last = grad_down
    grad_up = None
    columns = []
    for s in range(SPLITS):
        kept, gone, _ = lax.optimization_barrier((kepts[s], gones[s], last))
        total = kept + gone.astype(F32)
        blocks = [total[at * mine : (at + 1) * mine] for at in range(nz)]
        sends = [b.astype(BF16) for b in blocks[1:]]
        columns.append((blocks[0], [shift(b, -k) for k, b in zip(order[1:], sends)]))
        grad_up = up_pass(tied(delta, *sends), all_tokens, s, SPLITS, grad_up)
        last = grad_up
    done = []
    for first, rest in columns:
        for block in rest:
            first = first + block.astype(F32)
        done.append(first.astype(BF16))
    return (jnp.concatenate(done, axis=1), grad_up, grad_down)


def whole_plan(tokens, up_weight, down_weight, cotangent):
    gathered = functools.partial(lax.all_gather, axis_name="row", axis=0, tiled=True)
    panel_tokens, panel_cotangent = gathered(tokens), gathered(cotangent)
    pre_part = jnp.dot(panel_tokens, up_weight, preferred_element_type=F32)
    back_part = lax.dot_general(
        panel_cotangent, down_weight, NT, preferred_element_type=F32
    )
    preact, back_grad = lax.psum((pre_part, back_part), "col")
    activated, factor = gelu_parts(preact)
    activated = activated.astype(BF16)
    delta = (back_grad * factor).astype(BF16)
    grad_down = lax.dot_general(
        activated, panel_cotangent, TN, preferred_element_type=F32
    )
    grad_up = lax.dot_general(panel_tokens, delta, TN, preferred_element_type=F32)
    grad_input = lax.psum_scatter(
        lax.dot_general(delta, up_weight, NT, preferred_element_type=F32),
        "row",
        scatter_dimension=0,
        tiled=True,
    )
    return (grad_input.astype(BF16), grad_up.astype(BF16), grad_down.astype(BF16))


def solution(mesh):
    row, col = mesh.shape["row"], mesh.shape["col"]

    def per_device(tokens, up_weight, down_weight, cotangent):
        args = (tokens, up_weight, down_weight, cotangent)
        short = row == 8 and tokens.shape[0] % 16 == 0
        if col == 2 and short:
            return split_plan(row, *args)
        return whole_plan(*args)

    in_specs = (
        P(("groups", "row"), "col"),
        P("col", "row"),
        P("row", "col"),
        P(("groups", "row"), "col"),
    )
    out_specs = (
        P(("groups", "row"), "col"),
        P(("groups", "col"), "row"),
        P(("groups", "row"), "col"),
    )
    return jax.shard_map(
        per_device, mesh=mesh, in_specs=in_specs, out_specs=out_specs, check_vma=False
    )
```

```python
import functools

import jax
import jax.numpy as jnp
from jax import lax
from jax.experimental import pallas as pl
from jax.experimental.pallas import tpu as pltpu
from jax.sharding import PartitionSpec as P

F32 = jnp.float32
BF16 = jnp.bfloat16
VMEM_LIMIT = 36 * 1024 * 1024
NX = 2
PARTS = 2
SPLITS = 2
Z_AHEAD = 3
X_AHEAD = 2
PRE_TILE = 512
BACK_TILE = 512
IN_TILE = 256
NT = (((1,), (1,)), ((), ()))
TN = (((0,), (0,)), ((), ()))


def gelu_parts(preact):
    square = preact * preact
    curve_term = jnp.tanh(preact * (0.7978845608 + (0.7978845608 * 0.044715) * square))
    gate = 0.5 + 0.5 * curve_term
    slope = 0.5 * 0.7978845608 + (1.5 * 0.044715 * 0.7978845608) * square
    factor = gate + preact * (1.0 - curve_term * curve_term) * slope
    return (preact * gate, factor)


def params():
    return pltpu.CompilerParams(vmem_limit_bytes=VMEM_LIMIT)


def cost(flops, moved, weight=1):
    return pl.CostEstimate(
        flops=flops * weight // 20,
        bytes_accessed=moved * weight // 20,
        transcendentals=0,
    )


def joined(refs):
    return jnp.concatenate([r[...] for r in refs], axis=0)


def call(kernel, steps, in_specs, out_specs, out_shape, estimate, args, scratch=()):
    return pl.pallas_call(
        kernel,
        grid=(steps,),
        in_specs=in_specs,
        out_specs=out_specs,
        out_shape=out_shape,
        scratch_shapes=list(scratch),
        compiler_params=params(),
        cost_estimate=estimate,
    )(*args)


def whole(x):
    return pl.BlockSpec(x.shape, lambda i: (0, 0))


def pre_pass(tokens, up, first, hidden, weight):
    n = len(tokens)
    rows, feats = tokens[0].shape
    m = n * rows
    tile = min(PRE_TILE, hidden)
    base = first // tile

    def kernel(*refs):
        up_ref, out_ref = refs[n:]
        out_ref[...] = jnp.dot(
            joined(refs[:n]), up_ref[...], preferred_element_type=F32
        ).astype(BF16)

    return call(
        kernel,
        hidden // tile,
        [whole(t) for t in tokens]
        + [pl.BlockSpec((feats, tile), lambda i: (0, base + i))],
        pl.BlockSpec((m, tile), lambda i: (0, i)),
        jax.ShapeDtypeStruct((m, hidden), BF16),
        cost(2 * m * feats * hidden, 2 * feats * hidden + m * (2 * feats + 2 * hidden), weight),
        (*tokens, up),
    )


def back_pass(cots, down, pre, pre_other, first, weight):
    n = len(cots)
    rows, feats = cots[0].shape
    m, hidden = pre.shape
    tile = min(BACK_TILE, hidden)
    base = first // tile

    def kernel(*refs):
        down_ref, pre_ref, pre2_ref, act_ref, delta_ref = refs[n:]
        back = lax.dot_general(
            joined(refs[:n]), down_ref[...], NT, preferred_element_type=F32
        )
        activated, factor = gelu_parts(
            pre_ref[...].astype(F32) + pre2_ref[...].astype(F32)
        )
        act_ref[...] = activated.astype(BF16)
        delta_ref[...] = (back * factor).astype(BF16)

    column = pl.BlockSpec((m, tile), lambda i: (0, i))
    return call(
        kernel,
        hidden // tile,
        [whole(c) for c in cots]
        + [pl.BlockSpec((tile, feats), lambda i: (base + i, 0)), column, column],
        [column, column],
        [jax.ShapeDtypeStruct((m, hidden), BF16)] * 2,
        cost(
            2 * m * feats * hidden,
            2 * feats * hidden + m * (2 * feats + 8 * hidden),
            weight,
        ),
        (*cots, down, pre, pre_other),
    )


def summed(left, right):
    return (left.astype(F32) + right.astype(F32)).astype(BF16)


def input_pass(deltas, up, first, count):
    parts = len(deltas) // 2
    m, each = deltas[0].shape
    hidden = max(parts, 1) * each
    tile = min(IN_TILE, count)
    base = first // tile
    keep = m // NX

    def kernel(*refs):
        up_ref, keep_ref, send_ref = refs[len(deltas) : len(deltas) + 3]
        if parts:
            total_ref = refs[-1]

            @pl.when(pl.program_id(0) == 0)
            def _():
                for p in range(parts):
                    total_ref[:, p * each : (p + 1) * each] = summed(
                        refs[p][...], refs[parts + p][...]
                    )

        else:
            total_ref = refs[0]
        out = lax.dot_general(
            total_ref[...], up_ref[...], NT, preferred_element_type=F32
        )
        keep_ref[...] = out[:keep]
        send_ref[...] = out[keep:].astype(BF16)

    out_specs = [
        pl.BlockSpec((keep, tile), lambda i: (0, i)),
        pl.BlockSpec((m - keep, tile), lambda i: (0, i)),
    ]
    out_shape = [
        jax.ShapeDtypeStruct((keep, count), F32),
        jax.ShapeDtypeStruct((m - keep, count), BF16),
    ]
    if parts:
        out_specs.append(pl.BlockSpec((m, hidden), lambda i: (0, 0)))
        out_shape.append(jax.ShapeDtypeStruct((m, hidden), BF16))
    got = call(
        kernel,
        count // tile,
        [whole(d) for d in deltas]
        + [pl.BlockSpec((tile, hidden), lambda i: (base + i, 0))],
        out_specs,
        out_shape,
        cost(2 * m * hidden * count, 2 * count * hidden + 4 * m * hidden),
        (*deltas, up),
    )
    return got if parts else (*got, deltas[0])


def down_pass(act, cots, part, parts, into=None):
    n = len(cots)
    m, each = act.shape
    rows, feats = cots[0].shape
    tile = min(512, each)
    steps = each // tile
    extra = [] if into is None else [into]

    def kernel(*refs):
        refs[-1][...] = lax.dot_general(
            refs[0][...], joined(refs[1 : 1 + n]), TN, preferred_element_type=F32
        ).astype(BF16)

    return pl.pallas_call(
        kernel,
        grid=(steps,),
        in_specs=[pl.BlockSpec((m, tile), lambda i: (0, i))]
        + [whole(c) for c in cots]
        + [pl.BlockSpec(memory_space=pl.ANY)] * len(extra),
        out_specs=pl.BlockSpec((tile, feats), lambda i: (part * steps + i, 0)),
        out_shape=jax.ShapeDtypeStruct((parts * each, feats), BF16),
        input_output_aliases={1 + n: 0} if extra else {},
        compiler_params=params(),
        cost_estimate=cost(
            2 * m * each * feats, 2 * each * feats + 2 * m * (each + feats)
        ),
    )(act, *cots, *extra)


def up_pass(delta, tokens, part, parts, into=None):
    n = len(tokens)
    m, hidden = delta.shape
    rows, feats = tokens[0].shape
    each = hidden // parts
    tile = min(512, each)
    steps = each // tile
    extra = [] if into is None else [into]

    def kernel(*refs):
        refs[-1][...] = lax.dot_general(
            joined(refs[1 : 1 + n]), refs[0][...], TN, preferred_element_type=F32
        ).astype(BF16)

    return pl.pallas_call(
        kernel,
        grid=(steps,),
        in_specs=[pl.BlockSpec((m, tile), lambda i: (0, part * steps + i))]
        + [whole(t) for t in tokens]
        + [pl.BlockSpec(memory_space=pl.ANY)] * len(extra),
        out_specs=pl.BlockSpec((feats, tile), lambda i: (0, part * steps + i)),
        out_shape=jax.ShapeDtypeStruct((feats, hidden), BF16),
        input_output_aliases={1 + n: 0} if extra else {},
        compiler_params=params(),
        cost_estimate=cost(
            2 * m * each * feats, 2 * each * feats + 2 * m * (each + feats)
        ),
    )(delta, *tokens, *extra)


def tied(x, *after):
    return lax.optimization_barrier((x,) + after)[0] if after else x


def split_plan(row, tokens, up_weight, down_weight, cotangent):
    nz = row // NX
    mine, feats = tokens.shape

    def swap(x):
        return lax.ppermute(x, "col", [(0, 1), (1, 0)])

    def across(x):
        return lax.ppermute(x, "row", [(r, r ^ 1) for r in range(row)])

    def shift(x, k):
        return lax.ppermute(x, "row", [(r, (r + k * NX) % row) for r in range(row)])

    order = [0] + [k for j in range(1, nz // 2 + 1) for k in sorted({j, nz - j})]
    near, far = order[1:-1], order[-1]
    same = {("t", 0): tokens, ("c", 0): cotangent}
    facing, sent, crossed = {}, [], []
    for name, block, ks in (
        ("t", tokens, near + [far]),
        ("c", cotangent, near + [far]),
    ):
        for k in ks:
            tie = [same["t", far]] if name == "c" else []
            same[name, k] = shift(tied(block, *tie), k)
            sent.append(same[name, k])
    queue = [("t", 0), ("t", near[0]), ("c", 0)]
    queue += [("t", k) for k in near[1:] + [far]]
    queue += [("c", k) for k in near + [far]]
    for at in queue:
        tie = crossed[-X_AHEAD:][:1] if len(crossed) >= X_AHEAD else ()
        facing[at] = across(tied(same[at], *tie))
        crossed.append(facing[at])

    def pieces(name):
        return [same[name, k] for k in order] + [facing[name, k] for k in order]

    def after(blocks, *events):
        return [tied(blocks[0], *events)] + list(blocks[1:])

    hidden = up_weight.shape[1]
    each = hidden // 2
    all_tokens, all_cots = pieces("t"), pieces("c")
    pre0 = pre_pass(after(all_tokens, same["c", near[0]], same["c", near[1]]), up_weight, 0, each, 1)
    events = [pre0, *[same["c", k] for k in near+[far]], facing["c", near[0]], facing["c", near[1]]]
    pre1 = pre_pass(after(all_tokens, *events), up_weight, each, each, 100)
    other0, other1 = swap(pre0), swap(pre1)
    act0, delta0 = back_pass(after(all_cots, pre1), down_weight, pre0, other0, 0, 100)
    act1, delta1 = back_pass(after(all_cots, delta0), down_weight, pre1, other1, each, 1)
    deltas = [delta0, delta1, swap(delta0), swap(delta1)]
    grad_down = down_pass(tied(act0, delta1), all_cots, 0, 2)

    width = feats // SPLITS
    kepts, gones = [], []
    last = grad_down
    for s in range(SPLITS):
        kept, gone, delta = input_pass(
            after(deltas, last), up_weight, s * width, width
        )
        deltas, last = [delta], kept
        kepts.append(kept)
        gones.append(across(gone))
    grad_down = down_pass(tied(act1, last), all_cots, 1, 2, grad_down)
    last = grad_down
    grad_up = None
    columns = []
    for s in range(SPLITS):
        kept, gone, _ = lax.optimization_barrier((kepts[s], gones[s], last))
        total = kept + gone.astype(F32)
        blocks = [total[at * mine : (at + 1) * mine] for at in range(nz)]
        sends = [b.astype(BF16) for b in blocks[1:]]
        if columns:
            sends[0] = tied(sends[0], columns[-1][1][0])
        columns.append((blocks[0], [shift(b, -k) for k, b in zip(order[1:], sends)]))
        grad_up = up_pass(tied(delta, *sends), all_tokens, s, SPLITS, grad_up)
        last = grad_up
    done = []
    for first, rest in columns:
        first = tied(first, grad_up)
        for block in rest:
            first = first + block.astype(F32)
        done.append(first.astype(BF16))
    return (jnp.concatenate(done, axis=1), grad_up, grad_down)


def whole_plan(tokens, up_weight, down_weight, cotangent):
    gathered = functools.partial(lax.all_gather, axis_name="row", axis=0, tiled=True)
    panel_tokens, panel_cotangent = gathered(tokens), gathered(cotangent)
    pre_part = jnp.dot(panel_tokens, up_weight, preferred_element_type=F32)
    back_part = lax.dot_general(
        panel_cotangent, down_weight, NT, preferred_element_type=F32
    )
    preact, back_grad = lax.psum((pre_part, back_part), "col")
    activated, factor = gelu_parts(preact)
    activated = activated.astype(BF16)
    delta = (back_grad * factor).astype(BF16)
    grad_down = lax.dot_general(
        activated, panel_cotangent, TN, preferred_element_type=F32
    )
    grad_up = lax.dot_general(panel_tokens, delta, TN, preferred_element_type=F32)
    grad_input = lax.psum_scatter(
        lax.dot_general(delta, up_weight, NT, preferred_element_type=F32),
        "row",
        scatter_dimension=0,
        tiled=True,
    )
    return (grad_input.astype(BF16), grad_up.astype(BF16), grad_down.astype(BF16))


def solution(mesh):
    row, col = mesh.shape["row"], mesh.shape["col"]

    def per_device(tokens, up_weight, down_weight, cotangent):
        args = (tokens, up_weight, down_weight, cotangent)
        short = row == 8 and tokens.shape[0] % 16 == 0
        if col == 2 and short:
            return split_plan(row, *args)
        return whole_plan(*args)

    in_specs = (
        P(("groups", "row"), "col"),
        P("col", "row"),
        P("row", "col"),
        P(("groups", "row"), "col"),
    )
    out_specs = (
        P(("groups", "row"), "col"),
        P(("groups", "col"), "row"),
        P(("groups", "row"), "col"),
    )
    return jax.shard_map(
        per_device, mesh=mesh, in_specs=in_specs, out_specs=out_specs, check_vma=False
    )
```

```python
import functools

import jax
import jax.numpy as jnp
from jax import lax
from jax.experimental import pallas as pl
from jax.experimental.pallas import tpu as pltpu
from jax.sharding import PartitionSpec as P

F32 = jnp.float32
BF16 = jnp.bfloat16
NX = 2
PARTS = 2
SPLITS = 2
Z_AHEAD = 3
X_AHEAD = 2
PRE_TILE = 512
BACK_TILE = 512
IN_TILE = 512
NT = (((1,), (1,)), ((), ()))
TN = (((0,), (0,)), ((), ()))


def gelu_parts(preact):
    square = preact * preact
    curve_term = jnp.tanh(preact * (0.7978845608 + (0.7978845608 * 0.044715) * square))
    gate = 0.5 + 0.5 * curve_term
    slope = 0.5 * 0.7978845608 + (1.5 * 0.044715 * 0.7978845608) * square
    factor = gate + preact * (1.0 - curve_term * curve_term) * slope
    return (preact * gate, factor)


def params(mib=36):
    return pltpu.CompilerParams(vmem_limit_bytes=mib * 1024 * 1024)


def cost(flops, moved, weight=1):
    return pl.CostEstimate(
        flops=flops * weight // 20,
        bytes_accessed=moved * weight // 20,
        transcendentals=0,
    )


def joined(refs):
    return jnp.concatenate([r[...] for r in refs], axis=0)


def call(
    kernel, steps, in_specs, out_specs, out_shape, estimate, args, scratch=(), mib=36
):
    return pl.pallas_call(
        kernel,
        grid=(steps,),
        in_specs=in_specs,
        out_specs=out_specs,
        out_shape=out_shape,
        scratch_shapes=list(scratch),
        compiler_params=params(mib),
        cost_estimate=estimate,
    )(*args)


def whole(x):
    return pl.BlockSpec(x.shape, lambda i: (0, 0))


def pre_pass(tokens, up, first, hidden, weight):
    n = len(tokens)
    rows, feats = tokens[0].shape
    m = n * rows
    tile = min(PRE_TILE, hidden)
    base = first // tile

    def kernel(*refs):
        up_ref, out_ref = refs[n:]
        out_ref[...] = jnp.dot(
            joined(refs[:n]), up_ref[...], preferred_element_type=F32
        ).astype(BF16)

    return call(
        kernel,
        hidden // tile,
        [whole(t) for t in tokens]
        + [pl.BlockSpec((feats, tile), lambda i: (0, base + i))],
        pl.BlockSpec((m, tile), lambda i: (0, i)),
        jax.ShapeDtypeStruct((m, hidden), BF16),
        cost(2 * m * feats * hidden, 2 * feats * hidden + m * (2 * feats + 2 * hidden), weight),
        (*tokens, up),
    )


def back_pass(cots, down, pre, pre_other, first, weight):
    n = len(cots)
    rows, feats = cots[0].shape
    m, hidden = pre.shape
    tile = min(BACK_TILE, hidden)
    base = first // tile

    def kernel(*refs):
        down_ref, pre_ref, pre2_ref, act_ref, delta_ref = refs[n:]
        back = lax.dot_general(
            joined(refs[:n]), down_ref[...], NT, preferred_element_type=F32
        )
        activated, factor = gelu_parts(
            pre_ref[...].astype(F32) + pre2_ref[...].astype(F32)
        )
        act_ref[...] = activated.astype(BF16)
        delta_ref[...] = (back * factor).astype(BF16)

    column = pl.BlockSpec((m, tile), lambda i: (0, i))
    return call(
        kernel,
        hidden // tile,
        [whole(c) for c in cots]
        + [pl.BlockSpec((tile, feats), lambda i: (base + i, 0)), column, column],
        [column, column],
        [jax.ShapeDtypeStruct((m, hidden), BF16)] * 2,
        cost(
            2 * m * feats * hidden,
            2 * feats * hidden + m * (2 * feats + 8 * hidden),
            weight,
        ),
        (*cots, down, pre, pre_other),
    )


def summed(left, right):
    return (left.astype(F32) + right.astype(F32)).astype(BF16)


def input_pass(deltas, up, first, count):
    parts = len(deltas) // 2
    m, each = deltas[0].shape
    hidden = max(parts, 1) * each
    tile = min(IN_TILE, count)
    base = first // tile
    keep = m // NX

    def kernel(*refs):
        up_ref, keep_ref, send_ref = refs[len(deltas) : len(deltas) + 3]
        if parts:
            total_ref = refs[-1]

            @pl.when(pl.program_id(0) == 0)
            def _():
                for p in range(parts):
                    total_ref[:, p * each : (p + 1) * each] = summed(
                        refs[p][...], refs[parts + p][...]
                    )

        else:
            total_ref = refs[0]
        out = lax.dot_general(
            total_ref[...], up_ref[...], NT, preferred_element_type=F32
        )
        keep_ref[...] = out[:keep]
        send_ref[...] = out[keep:].astype(BF16)

    out_specs = [
        pl.BlockSpec((keep, tile), lambda i: (0, i)),
        pl.BlockSpec((m - keep, tile), lambda i: (0, i)),
    ]
    out_shape = [
        jax.ShapeDtypeStruct((keep, count), F32),
        jax.ShapeDtypeStruct((m - keep, count), BF16),
    ]
    if parts:
        out_specs.append(pl.BlockSpec((m, hidden), lambda i: (0, 0)))
        out_shape.append(jax.ShapeDtypeStruct((m, hidden), BF16))
    got = call(
        kernel,
        count // tile,
        [whole(d) for d in deltas]
        + [pl.BlockSpec((tile, hidden), lambda i: (base + i, 0))],
        out_specs,
        out_shape,
        cost(2 * m * hidden * count, 2 * count * hidden + 4 * m * hidden),
        (*deltas, up),
        mib=24,
    )
    return got if parts else (*got, deltas[0])


def down_pass(act, cots, part, parts, into=None):
    n = len(cots)
    m, each = act.shape
    rows, feats = cots[0].shape
    tile = min(512, each)
    steps = each // tile
    extra = [] if into is None else [into]

    def kernel(*refs):
        refs[-1][...] = lax.dot_general(
            refs[0][...], joined(refs[1 : 1 + n]), TN, preferred_element_type=F32
        ).astype(BF16)

    return pl.pallas_call(
        kernel,
        grid=(steps,),
        in_specs=[pl.BlockSpec((m, tile), lambda i: (0, i))]
        + [whole(c) for c in cots]
        + [pl.BlockSpec(memory_space=pl.ANY)] * len(extra),
        out_specs=pl.BlockSpec((tile, feats), lambda i: (part * steps + i, 0)),
        out_shape=jax.ShapeDtypeStruct((parts * each, feats), BF16),
        input_output_aliases={1 + n: 0} if extra else {},
        compiler_params=params(20),
        cost_estimate=cost(
            2 * m * each * feats,
            2 * each * feats + 2 * m * (each + feats),
            60 if into is None else 1,
        ),
    )(act, *cots, *extra)


def up_pass(delta, tokens, part, parts, into=None):
    n = len(tokens)
    m, hidden = delta.shape
    rows, feats = tokens[0].shape
    each = hidden // parts
    tile = min(512, each)
    steps = each // tile
    extra = [] if into is None else [into]

    def kernel(*refs):
        refs[-1][...] = lax.dot_general(
            joined(refs[1 : 1 + n]), refs[0][...], TN, preferred_element_type=F32
        ).astype(BF16)

    return pl.pallas_call(
        kernel,
        grid=(steps,),
        in_specs=[pl.BlockSpec((m, tile), lambda i: (0, part * steps + i))]
        + [whole(t) for t in tokens]
        + [pl.BlockSpec(memory_space=pl.ANY)] * len(extra),
        out_specs=pl.BlockSpec((feats, tile), lambda i: (0, part * steps + i)),
        out_shape=jax.ShapeDtypeStruct((feats, hidden), BF16),
        input_output_aliases={1 + n: 0} if extra else {},
        compiler_params=params(36),
        cost_estimate=cost(
            2 * m * each * feats, 2 * each * feats + 2 * m * (each + feats)
        ),
    )(delta, *tokens, *extra)


def tied(x, *after):
    return lax.optimization_barrier((x,) + after)[0] if after else x


def split_plan(row, tokens, up_weight, down_weight, cotangent):
    nz = row // NX
    mine, feats = tokens.shape

    def swap(x):
        return lax.ppermute(x, "col", [(0, 1), (1, 0)])

    def across(x):
        return lax.ppermute(x, "row", [(r, r ^ 1) for r in range(row)])

    def shift(x, k):
        return lax.ppermute(x, "row", [(r, (r + k * NX) % row) for r in range(row)])

    order = [0] + [k for j in range(1, nz // 2 + 1) for k in sorted({j, nz - j})]
    near, far = order[1:-1], order[-1]
    same = {("t", 0): tokens, ("c", 0): cotangent}
    facing, sent, crossed = {}, [], []
    for name, block, ks in (
        ("t", tokens, near + [far]),
        ("c", cotangent, near + [far]),
    ):
        for k in ks:
            tie = [same["t", far]] if name == "c" else []
            same[name, k] = shift(tied(block, *tie), k)
            sent.append(same[name, k])
    queue = [("t", 0), ("t", near[0]), ("c", 0)]
    queue += [("t", k) for k in near[1:] + [far]]
    queue += [("c", k) for k in near + [far]]
    for at in queue:
        tie = crossed[-X_AHEAD:][:1] if len(crossed) >= X_AHEAD else ()
        facing[at] = across(tied(same[at], *tie))
        crossed.append(facing[at])

    def pieces(name):
        return [same[name, k] for k in order] + [facing[name, k] for k in order]

    def after(blocks, *events):
        return [tied(blocks[0], *events)] + list(blocks[1:])

    hidden = up_weight.shape[1]
    each = hidden // 2
    all_tokens, all_cots = pieces("t"), pieces("c")
    pre0 = pre_pass(after(all_tokens, same["c", near[0]], same["c", near[1]]), up_weight, 0, each, 1)
    events = [pre0, *[same["c", k] for k in near+[far]], facing["c", near[0]], facing["c", near[1]]]
    pre1 = pre_pass(after(all_tokens, *events), up_weight, each, each, 100)
    other0, other1 = swap(pre0), swap(pre1)
    act0, delta0 = back_pass(after(all_cots, pre1), down_weight, pre0, other0, 0, 100)
    act1, delta1 = back_pass(after(all_cots, delta0), down_weight, pre1, other1, each, 1)
    deltas = [delta0, delta1, swap(delta0), swap(delta1)]
    grad_down = down_pass(tied(act0, delta1), all_cots, 0, 2)

    width = feats // SPLITS
    kepts, gones = [], []
    last = grad_down
    for s in range(SPLITS):
        kept, gone, delta = input_pass(
            after(deltas, last), up_weight, s * width, width
        )
        deltas, last = [delta], kept
        kepts.append(kept)
        gones.append(across(gone))
    grad_down = down_pass(tied(act1, last), all_cots, 1, 2, grad_down)
    last = grad_down
    grad_up = None
    columns = []
    for s in range(SPLITS):
        kept, gone, _ = lax.optimization_barrier((kepts[s], gones[s], last))
        total = kept + gone.astype(F32)
        blocks = [total[at * mine : (at + 1) * mine] for at in range(nz)]
        sends = [b.astype(BF16) for b in blocks[1:]]
        if columns:
            sends[0] = tied(sends[0], columns[-1][1][0])
        columns.append((blocks[0], [shift(b, -k) for k, b in zip(order[1:], sends)]))
        grad_up = up_pass(tied(delta, *sends), all_tokens, s, SPLITS, grad_up)
        last = grad_up
    done = []
    for first, rest in columns:
        first = tied(first, grad_up)
        for block in rest:
            first = first + block.astype(F32)
        done.append(first.astype(BF16))
    return (jnp.concatenate(done, axis=1), grad_up, grad_down)


def whole_plan(tokens, up_weight, down_weight, cotangent):
    gathered = functools.partial(lax.all_gather, axis_name="row", axis=0, tiled=True)
    panel_tokens, panel_cotangent = gathered(tokens), gathered(cotangent)
    pre_part = jnp.dot(panel_tokens, up_weight, preferred_element_type=F32)
    back_part = lax.dot_general(
        panel_cotangent, down_weight, NT, preferred_element_type=F32
    )
    preact, back_grad = lax.psum((pre_part, back_part), "col")
    activated, factor = gelu_parts(preact)
    activated = activated.astype(BF16)
    delta = (back_grad * factor).astype(BF16)
    grad_down = lax.dot_general(
        activated, panel_cotangent, TN, preferred_element_type=F32
    )
    grad_up = lax.dot_general(panel_tokens, delta, TN, preferred_element_type=F32)
    grad_input = lax.psum_scatter(
        lax.dot_general(delta, up_weight, NT, preferred_element_type=F32),
        "row",
        scatter_dimension=0,
        tiled=True,
    )
    return (grad_input.astype(BF16), grad_up.astype(BF16), grad_down.astype(BF16))


def solution(mesh):
    row, col = mesh.shape["row"], mesh.shape["col"]

    def per_device(tokens, up_weight, down_weight, cotangent):
        args = (tokens, up_weight, down_weight, cotangent)
        short = row == 8 and tokens.shape[0] % 16 == 0
        if col == 2 and short:
            return split_plan(row, *args)
        return whole_plan(*args)

    in_specs = (
        P(("groups", "row"), "col"),
        P("col", "row"),
        P("row", "col"),
        P(("groups", "row"), "col"),
    )
    out_specs = (
        P(("groups", "row"), "col"),
        P(("groups", "col"), "row"),
        P(("groups", "row"), "col"),
    )
    return jax.shard_map(
        per_device, mesh=mesh, in_specs=in_specs, out_specs=out_specs, check_vma=False
    )
```

```python
import functools

import jax
import jax.numpy as jnp
from jax import lax
from jax.experimental import pallas as pl
from jax.experimental.pallas import tpu as pltpu
from jax.sharding import PartitionSpec as P

F32 = jnp.float32
BF16 = jnp.bfloat16
NX = 2
PARTS = 2
SPLITS = 2
Z_AHEAD = 3
X_AHEAD = 2
PRE_TILE = 1024
BACK_TILE = 512
IN_TILE = 512
NT = (((1,), (1,)), ((), ()))
TN = (((0,), (0,)), ((), ()))


def gelu_parts(preact):
    square = preact * preact
    curve_term = jnp.tanh(preact * (0.7978845608 + (0.7978845608 * 0.044715) * square))
    gate = 0.5 + 0.5 * curve_term
    slope = 0.5 * 0.7978845608 + (1.5 * 0.044715 * 0.7978845608) * square
    factor = gate + preact * (1.0 - curve_term * curve_term) * slope
    return (preact * gate, factor)


def params(mib=36):
    return pltpu.CompilerParams(vmem_limit_bytes=mib * 1024 * 1024)


def cost(flops, moved, weight=1):
    return pl.CostEstimate(
        flops=flops * weight // 20,
        bytes_accessed=moved * weight // 20,
        transcendentals=0,
    )


def joined(refs):
    return jnp.concatenate([r[...] for r in refs], axis=0)


def call(
    kernel, steps, in_specs, out_specs, out_shape, estimate, args, scratch=(), mib=36
):
    return pl.pallas_call(
        kernel,
        grid=(steps,),
        in_specs=in_specs,
        out_specs=out_specs,
        out_shape=out_shape,
        scratch_shapes=list(scratch),
        compiler_params=params(mib),
        cost_estimate=estimate,
    )(*args)


def whole(x):
    return pl.BlockSpec(x.shape, lambda i: (0, 0))


def pre_pass(tokens, up, first, hidden, weight):
    n = len(tokens)
    rows, feats = tokens[0].shape
    m = n * rows
    tile = min(PRE_TILE, hidden)
    base = first // tile

    def kernel(*refs):
        up_ref, out_ref = refs[n:]
        out_ref[...] = jnp.dot(
            joined(refs[:n]), up_ref[...], preferred_element_type=F32
        ).astype(BF16)

    return call(
        kernel,
        hidden // tile,
        [whole(t) for t in tokens]
        + [pl.BlockSpec((feats, tile), lambda i: (0, base + i))],
        pl.BlockSpec((m, tile), lambda i: (0, i)),
        jax.ShapeDtypeStruct((m, hidden), BF16),
        cost(2 * m * feats * hidden, 2 * feats * hidden + m * (2 * feats + 2 * hidden), weight),
        (*tokens, up),
    )


def back_pass(cots, down, pre, pre_other, first, weight):
    n = len(cots)
    rows, feats = cots[0].shape
    m, hidden = pre.shape
    tile = min(BACK_TILE, hidden)
    base = first // tile

    def kernel(*refs):
        down_ref, pre_ref, pre2_ref, act_ref, delta_ref = refs[n:]
        back = lax.dot_general(
            joined(refs[:n]), down_ref[...], NT, preferred_element_type=F32
        )
        activated, factor = gelu_parts(
            pre_ref[...].astype(F32) + pre2_ref[...].astype(F32)
        )
        act_ref[...] = activated.astype(BF16)
        delta_ref[...] = (back * factor).astype(BF16)

    column = pl.BlockSpec((m, tile), lambda i: (0, i))
    return call(
        kernel,
        hidden // tile,
        [whole(c) for c in cots]
        + [pl.BlockSpec((tile, feats), lambda i: (base + i, 0)), column, column],
        [column, column],
        [jax.ShapeDtypeStruct((m, hidden), BF16)] * 2,
        cost(
            2 * m * feats * hidden,
            2 * feats * hidden + m * (2 * feats + 8 * hidden),
            weight,
        ),
        (*cots, down, pre, pre_other),
    )


def summed(left, right):
    return (left.astype(F32) + right.astype(F32)).astype(BF16)


def input_pass(deltas, up, first, count):
    parts = len(deltas) // 2
    m, each = deltas[0].shape
    hidden = max(parts, 1) * each
    tile = min(IN_TILE, count)
    base = first // tile
    keep = m // NX

    def kernel(*refs):
        up_ref, keep_ref, send_ref = refs[len(deltas) : len(deltas) + 3]
        if parts:
            total_ref = refs[-1]

            @pl.when(pl.program_id(0) == 0)
            def _():
                for p in range(parts):
                    total_ref[:, p * each : (p + 1) * each] = summed(
                        refs[p][...], refs[parts + p][...]
                    )

        else:
            total_ref = refs[0]
        out = lax.dot_general(
            total_ref[...], up_ref[...], NT, preferred_element_type=F32
        )
        keep_ref[...] = out[:keep]
        send_ref[...] = out[keep:].astype(BF16)

    out_specs = [
        pl.BlockSpec((keep, tile), lambda i: (0, i)),
        pl.BlockSpec((m - keep, tile), lambda i: (0, i)),
    ]
    out_shape = [
        jax.ShapeDtypeStruct((keep, count), F32),
        jax.ShapeDtypeStruct((m - keep, count), BF16),
    ]
    if parts:
        out_specs.append(pl.BlockSpec((m, hidden), lambda i: (0, 0)))
        out_shape.append(jax.ShapeDtypeStruct((m, hidden), BF16))
    got = call(
        kernel,
        count // tile,
        [whole(d) for d in deltas]
        + [pl.BlockSpec((tile, hidden), lambda i: (base + i, 0))],
        out_specs,
        out_shape,
        cost(2 * m * hidden * count, 2 * count * hidden + 4 * m * hidden),
        (*deltas, up),
        mib=22,
    )
    return got if parts else (*got, deltas[0])


def down_pass(act, cots, part, parts, into=None):
    n = len(cots)
    m, each = act.shape
    rows, feats = cots[0].shape
    tile = min(512, each)
    steps = each // tile
    extra = [] if into is None else [into]

    def kernel(*refs):
        refs[-1][...] = lax.dot_general(
            refs[0][...], joined(refs[1 : 1 + n]), TN, preferred_element_type=F32
        ).astype(BF16)

    return pl.pallas_call(
        kernel,
        grid=(steps,),
        in_specs=[pl.BlockSpec((m, tile), lambda i: (0, i))]
        + [whole(c) for c in cots]
        + [pl.BlockSpec(memory_space=pl.ANY)] * len(extra),
        out_specs=pl.BlockSpec((tile, feats), lambda i: (part * steps + i, 0)),
        out_shape=jax.ShapeDtypeStruct((parts * each, feats), BF16),
        input_output_aliases={1 + n: 0} if extra else {},
        compiler_params=params(16),
        cost_estimate=cost(
            2 * m * each * feats,
            2 * each * feats + 2 * m * (each + feats),
            100 if into is None else 1,
        ),
    )(act, *cots, *extra)


def up_pass(delta, tokens, part, parts, into=None):
    n = len(tokens)
    m, hidden = delta.shape
    rows, feats = tokens[0].shape
    each = hidden // parts
    tile = min(512, each)
    steps = each // tile
    extra = [] if into is None else [into]

    def kernel(*refs):
        refs[-1][...] = lax.dot_general(
            joined(refs[1 : 1 + n]), refs[0][...], TN, preferred_element_type=F32
        ).astype(BF16)

    return pl.pallas_call(
        kernel,
        grid=(steps,),
        in_specs=[pl.BlockSpec((m, tile), lambda i: (0, part * steps + i))]
        + [whole(t) for t in tokens]
        + [pl.BlockSpec(memory_space=pl.ANY)] * len(extra),
        out_specs=pl.BlockSpec((feats, tile), lambda i: (0, part * steps + i)),
        out_shape=jax.ShapeDtypeStruct((feats, hidden), BF16),
        input_output_aliases={1 + n: 0} if extra else {},
        compiler_params=params(36),
        cost_estimate=cost(
            2 * m * each * feats, 2 * each * feats + 2 * m * (each + feats)
        ),
    )(delta, *tokens, *extra)


def tied(x, *after):
    return lax.optimization_barrier((x,) + after)[0] if after else x


def split_plan(row, tokens, up_weight, down_weight, cotangent):
    nz = row // NX
    mine, feats = tokens.shape

    def swap(x):
        return lax.ppermute(x, "col", [(0, 1), (1, 0)])

    def across(x):
        return lax.ppermute(x, "row", [(r, r ^ 1) for r in range(row)])

    def shift(x, k):
        return lax.ppermute(x, "row", [(r, (r + k * NX) % row) for r in range(row)])

    order = [0] + [k for j in range(1, nz // 2 + 1) for k in sorted({j, nz - j})]
    near, far = order[1:-1], order[-1]
    same = {("t", 0): tokens, ("c", 0): cotangent}
    facing, sent, crossed = {}, [], []
    for name, block, ks in (
        ("t", tokens, near + [far]),
        ("c", cotangent, near + [far]),
    ):
        for k in ks:
            tie = [same["t", far]] if name == "c" else []
            same[name, k] = shift(tied(block, *tie), k)
            sent.append(same[name, k])
    queue = [("t", 0), ("t", near[0]), ("c", 0)]
    queue += [("t", k) for k in near[1:] + [far]]
    queue += [("c", k) for k in near + [far]]
    for at in queue:
        tie = crossed[-X_AHEAD:][:1] if len(crossed) >= X_AHEAD else ()
        facing[at] = across(tied(same[at], *tie))
        crossed.append(facing[at])

    def pieces(name):
        return [same[name, k] for k in order] + [facing[name, k] for k in order]

    def after(blocks, *events):
        return [tied(blocks[0], *events)] + list(blocks[1:])

    hidden = up_weight.shape[1]
    each = hidden // 2
    all_tokens, all_cots = pieces("t"), pieces("c")
    pre0 = pre_pass(after(all_tokens, same["c", near[0]], same["c", near[1]]), up_weight, 0, each, 1)
    events = [pre0, *[same["c", k] for k in near+[far]], facing["c", near[0]], facing["c", near[1]]]
    pre1 = pre_pass(after(all_tokens, *events), up_weight, each, each, 100)
    other0, other1 = swap(pre0), swap(pre1)
    act0, delta0 = back_pass(after(all_cots, pre1), down_weight, pre0, other0, 0, 100)
    act1, delta1 = back_pass(after(all_cots, delta0), down_weight, pre1, other1, each, 1)
    deltas = [delta0, delta1, swap(delta0), swap(delta1)]
    grad_down = down_pass(tied(act0, delta1), all_cots, 0, 2)

    width = feats // SPLITS
    kepts, gones = [], []
    last = grad_down
    for s in range(SPLITS):
        kept, gone, delta = input_pass(
            after(deltas, last), up_weight, s * width, width
        )
        deltas, last = [delta], kept
        kepts.append(kept)
        gones.append(across(gone))
    grad_down = down_pass(tied(act1, last), all_cots, 1, 2, grad_down)
    last = grad_down
    grad_up = None
    columns = []
    for s in range(SPLITS):
        kept, gone, _ = lax.optimization_barrier((kepts[s], gones[s], last))
        total = kept + gone.astype(F32)
        blocks = [total[at * mine : (at + 1) * mine] for at in range(nz)]
        sends = [b.astype(BF16) for b in blocks[1:]]
        if columns:
            sends[0] = tied(sends[0], columns[-1][1][0])
        columns.append((blocks[0], [shift(b, -k) for k, b in zip(order[1:], sends)]))
        grad_up = up_pass(tied(delta, *sends), all_tokens, s, SPLITS, grad_up)
        last = grad_up
    done = []
    for first, rest in columns:
        first = tied(first, grad_up)
        for block in rest:
            first = first + block.astype(F32)
        done.append(first.astype(BF16))
    return (jnp.concatenate(done, axis=1), grad_up, grad_down)


def whole_plan(tokens, up_weight, down_weight, cotangent):
    gathered = functools.partial(lax.all_gather, axis_name="row", axis=0, tiled=True)
    panel_tokens, panel_cotangent = gathered(tokens), gathered(cotangent)
    pre_part = jnp.dot(panel_tokens, up_weight, preferred_element_type=F32)
    back_part = lax.dot_general(
        panel_cotangent, down_weight, NT, preferred_element_type=F32
    )
    preact, back_grad = lax.psum((pre_part, back_part), "col")
    activated, factor = gelu_parts(preact)
    activated = activated.astype(BF16)
    delta = (back_grad * factor).astype(BF16)
    grad_down = lax.dot_general(
        activated, panel_cotangent, TN, preferred_element_type=F32
    )
    grad_up = lax.dot_general(panel_tokens, delta, TN, preferred_element_type=F32)
    grad_input = lax.psum_scatter(
        lax.dot_general(delta, up_weight, NT, preferred_element_type=F32),
        "row",
        scatter_dimension=0,
        tiled=True,
    )
    return (grad_input.astype(BF16), grad_up.astype(BF16), grad_down.astype(BF16))


def solution(mesh):
    row, col = mesh.shape["row"], mesh.shape["col"]

    def per_device(tokens, up_weight, down_weight, cotangent):
        args = (tokens, up_weight, down_weight, cotangent)
        short = row == 8 and tokens.shape[0] % 16 == 0
        if col == 2 and short:
            return split_plan(row, *args)
        return whole_plan(*args)

    in_specs = (
        P(("groups", "row"), "col"),
        P("col", "row"),
        P("row", "col"),
        P(("groups", "row"), "col"),
    )
    out_specs = (
        P(("groups", "row"), "col"),
        P(("groups", "col"), "row"),
        P(("groups", "row"), "col"),
    )
    return jax.shard_map(
        per_device, mesh=mesh, in_specs=in_specs, out_specs=out_specs, check_vma=False
    )
```

```python
import functools

import jax
import jax.numpy as jnp
from jax import lax
from jax.experimental import pallas as pl
from jax.experimental.pallas import tpu as pltpu
from jax.sharding import PartitionSpec as P

F32 = jnp.float32
BF16 = jnp.bfloat16
NX = 2
PARTS = 2
SPLITS = 2
Z_AHEAD = 3
X_AHEAD = 2
PRE_TILE = 1024
BACK_TILE = 512
IN_TILE = 512
NT = (((1,), (1,)), ((), ()))
TN = (((0,), (0,)), ((), ()))


def gelu_parts(preact):
    square = preact * preact
    curve_term = jnp.tanh(preact * (0.7978845608 + (0.7978845608 * 0.044715) * square))
    gate = 0.5 + 0.5 * curve_term
    slope = 0.5 * 0.7978845608 + (1.5 * 0.044715 * 0.7978845608) * square
    factor = gate + preact * (1.0 - curve_term * curve_term) * slope
    return (preact * gate, factor)


def params(mib=36):
    return pltpu.CompilerParams(vmem_limit_bytes=mib * 1024 * 1024)


def cost(flops, moved, weight=1):
    return pl.CostEstimate(
        flops=flops * weight // 20,
        bytes_accessed=moved * weight // 20,
        transcendentals=0,
    )


def joined(refs):
    return jnp.concatenate([r[...] for r in refs], axis=0)


def call(
    kernel, steps, in_specs, out_specs, out_shape, estimate, args, scratch=(), mib=36
):
    return pl.pallas_call(
        kernel,
        grid=(steps,),
        in_specs=in_specs,
        out_specs=out_specs,
        out_shape=out_shape,
        scratch_shapes=list(scratch),
        compiler_params=params(mib),
        cost_estimate=estimate,
    )(*args)


def whole(x):
    return pl.BlockSpec(x.shape, lambda i: (0, 0))


def pre_pass(tokens, up, first, hidden, weight):
    n = len(tokens)
    rows, feats = tokens[0].shape
    m = n * rows
    tile = min(PRE_TILE, hidden)
    base = first // tile

    def kernel(*refs):
        up_ref, out_ref = refs[n:]
        out_ref[...] = jnp.dot(
            joined(refs[:n]), up_ref[...], preferred_element_type=F32
        ).astype(BF16)

    return call(
        kernel,
        hidden // tile,
        [whole(t) for t in tokens]
        + [pl.BlockSpec((feats, tile), lambda i: (0, base + i))],
        pl.BlockSpec((m, tile), lambda i: (0, i)),
        jax.ShapeDtypeStruct((m, hidden), BF16),
        cost(2 * m * feats * hidden, 2 * feats * hidden + m * (2 * feats + 2 * hidden), weight),
        (*tokens, up),
    )


def back_pass(cots, down, pre, pre_other, first, weight):
    n = len(cots)
    rows, feats = cots[0].shape
    m, hidden = pre.shape
    tile = min(BACK_TILE, hidden)
    base = first // tile

    def kernel(*refs):
        down_ref, pre_ref, pre2_ref, act_ref, delta_ref = refs[n:]
        back = lax.dot_general(
            joined(refs[:n]), down_ref[...], NT, preferred_element_type=F32
        )
        activated, factor = gelu_parts(
            pre_ref[...].astype(F32) + pre2_ref[...].astype(F32)
        )
        act_ref[...] = activated.astype(BF16)
        delta_ref[...] = (back * factor).astype(BF16)

    column = pl.BlockSpec((m, tile), lambda i: (0, i))
    return call(
        kernel,
        hidden // tile,
        [whole(c) for c in cots]
        + [pl.BlockSpec((tile, feats), lambda i: (base + i, 0)), column, column],
        [column, column],
        [jax.ShapeDtypeStruct((m, hidden), BF16)] * 2,
        cost(
            2 * m * feats * hidden,
            2 * feats * hidden + m * (2 * feats + 8 * hidden),
            weight,
        ),
        (*cots, down, pre, pre_other),
    )


def summed(left, right):
    return (left.astype(F32) + right.astype(F32)).astype(BF16)


def input_pass(deltas, up, first, count):
    parts = len(deltas) // 2
    m, each = deltas[0].shape
    hidden = max(parts, 1) * each
    tile = min(IN_TILE, count)
    base = first // tile
    keep = m // NX

    def kernel(*refs):
        up_ref, keep_ref, send_ref = refs[len(deltas) : len(deltas) + 3]
        if parts:
            total_ref = refs[-1]

            @pl.when(pl.program_id(0) == 0)
            def _():
                for p in range(parts):
                    total_ref[:, p * each : (p + 1) * each] = summed(
                        refs[p][...], refs[parts + p][...]
                    )

        else:
            total_ref = refs[0]
        out = lax.dot_general(
            total_ref[...], up_ref[...], NT, preferred_element_type=F32
        )
        keep_ref[...] = out[:keep]
        send_ref[...] = out[keep:].astype(BF16)

    out_specs = [
        pl.BlockSpec((keep, tile), lambda i: (0, i)),
        pl.BlockSpec((m - keep, tile), lambda i: (0, i)),
    ]
    out_shape = [
        jax.ShapeDtypeStruct((keep, count), F32),
        jax.ShapeDtypeStruct((m - keep, count), BF16),
    ]
    if parts:
        out_specs.append(pl.BlockSpec((m, hidden), lambda i: (0, 0)))
        out_shape.append(jax.ShapeDtypeStruct((m, hidden), BF16))
    got = call(
        kernel,
        count // tile,
        [whole(d) for d in deltas]
        + [pl.BlockSpec((tile, hidden), lambda i: (base + i, 0))],
        out_specs,
        out_shape,
        cost(2 * m * hidden * count, 2 * count * hidden + 4 * m * hidden),
        (*deltas, up),
        mib=22,
    )
    return got if parts else (*got, deltas[0])


def down_pass(act, cots, part, parts, into=None):
    n = len(cots)
    m, each = act.shape
    rows, feats = cots[0].shape
    tile = min(512, each)
    steps = each // tile
    extra = [] if into is None else [into]

    def kernel(*refs):
        refs[-1][...] = lax.dot_general(
            refs[0][...], joined(refs[1 : 1 + n]), TN, preferred_element_type=F32
        ).astype(BF16)

    return pl.pallas_call(
        kernel,
        grid=(steps,),
        in_specs=[pl.BlockSpec((m, tile), lambda i: (0, i))]
        + [whole(c) for c in cots]
        + [pl.BlockSpec(memory_space=pl.ANY)] * len(extra),
        out_specs=pl.BlockSpec((tile, feats), lambda i: (part * steps + i, 0)),
        out_shape=jax.ShapeDtypeStruct((parts * each, feats), BF16),
        input_output_aliases={1 + n: 0} if extra else {},
        compiler_params=params(16),
        cost_estimate=cost(
            2 * m * each * feats,
            2 * each * feats + 2 * m * (each + feats),
            100 if into is None else 1,
        ),
    )(act, *cots, *extra)


def up_pass(delta, tokens, part, parts, into=None):
    n = len(tokens)
    m, hidden = delta.shape
    rows, feats = tokens[0].shape
    each = hidden // parts
    tile = min(512, each)
    steps = each // tile
    extra = [] if into is None else [into]

    def kernel(*refs):
        refs[-1][...] = lax.dot_general(
            joined(refs[1 : 1 + n]), refs[0][...], TN, preferred_element_type=F32
        ).astype(BF16)

    return pl.pallas_call(
        kernel,
        grid=(steps,),
        in_specs=[pl.BlockSpec((m, tile), lambda i: (0, part * steps + i))]
        + [whole(t) for t in tokens]
        + [pl.BlockSpec(memory_space=pl.ANY)] * len(extra),
        out_specs=pl.BlockSpec((feats, tile), lambda i: (0, part * steps + i)),
        out_shape=jax.ShapeDtypeStruct((feats, hidden), BF16),
        input_output_aliases={1 + n: 0} if extra else {},
        compiler_params=params(24),
        cost_estimate=cost(
            2 * m * each * feats, 2 * each * feats + 2 * m * (each + feats)
        ),
    )(delta, *tokens, *extra)


def tied(x, *after):
    return lax.optimization_barrier((x,) + after)[0] if after else x


def split_plan(row, tokens, up_weight, down_weight, cotangent):
    nz = row // NX
    mine, feats = tokens.shape

    def swap(x):
        return lax.ppermute(x, "col", [(0, 1), (1, 0)])

    def across(x):
        return lax.ppermute(x, "row", [(r, r ^ 1) for r in range(row)])

    def shift(x, k):
        return lax.ppermute(x, "row", [(r, (r + k * NX) % row) for r in range(row)])

    order = [0] + [k for j in range(1, nz // 2 + 1) for k in sorted({j, nz - j})]
    near, far = order[1:-1], order[-1]
    same = {("t", 0): tokens, ("c", 0): cotangent}
    facing, sent, crossed = {}, [], []
    for name, block, ks in (
        ("t", tokens, near + [far]),
        ("c", cotangent, near + [far]),
    ):
        for k in ks:
            tie = [same["t", far]] if name == "c" else []
            same[name, k] = shift(tied(block, *tie), k)
            sent.append(same[name, k])
    queue = [("t", 0), ("t", near[0]), ("c", 0)]
    queue += [("t", k) for k in near[1:] + [far]]
    queue += [("c", k) for k in near + [far]]
    for at in queue:
        tie = crossed[-X_AHEAD:][:1] if len(crossed) >= X_AHEAD else ()
        facing[at] = across(tied(same[at], *tie))
        crossed.append(facing[at])

    def pieces(name):
        return [same[name, k] for k in order] + [facing[name, k] for k in order]

    def after(blocks, *events):
        return [tied(blocks[0], *events)] + list(blocks[1:])

    hidden = up_weight.shape[1]
    each = hidden // 2
    all_tokens, all_cots = pieces("t"), pieces("c")
    pre0 = pre_pass(after(all_tokens, same["c", near[0]], same["c", near[1]]), up_weight, 0, each, 1)
    events = [pre0, *[same["c", k] for k in near+[far]], facing["c", near[0]], facing["c", near[1]]]
    pre1 = pre_pass(after(all_tokens, *events), up_weight, each, each, 100)
    other0, other1 = swap(pre0), swap(pre1)
    act0, delta0 = back_pass(after(all_cots, pre1), down_weight, pre0, other0, 0, 100)
    act1, delta1 = back_pass(after(all_cots, delta0), down_weight, pre1, other1, each, 1)
    deltas = [delta0, delta1, swap(delta0), swap(delta1)]
    grad_down = down_pass(tied(act0, delta1), all_cots, 0, 2)

    width = feats // SPLITS
    kepts, gones = [], []
    last = grad_down
    for s in range(SPLITS):
        kept, gone, delta = input_pass(
            after(deltas, last), up_weight, s * width, width
        )
        deltas, last = [delta], kept
        kepts.append(kept)
        gones.append(across(gone))
    grad_down = down_pass(tied(act1, last), all_cots, 1, 2, grad_down)
    last = grad_down
    grad_up = None
    columns = []
    for s in range(SPLITS):
        kept, gone, _ = lax.optimization_barrier((kepts[s], gones[s], last))
        total = kept + gone.astype(F32)
        blocks = [total[at * mine : (at + 1) * mine] for at in range(nz)]
        sends = [b.astype(BF16) for b in blocks[1:]]
        if columns:
            sends[0] = tied(sends[0], columns[-1][1][1])
        columns.append((blocks[0], [shift(b, -k) for k, b in zip(order[1:], sends)]))
        grad_up = up_pass(tied(delta, *sends), all_tokens, s, SPLITS, grad_up)
        last = grad_up
    done = []
    for first, rest in columns:
        first = tied(first, grad_up)
        for block in rest:
            first = first + block.astype(F32)
        done.append(first.astype(BF16))
    return (jnp.concatenate(done, axis=1), grad_up, grad_down)


def whole_plan(tokens, up_weight, down_weight, cotangent):
    gathered = functools.partial(lax.all_gather, axis_name="row", axis=0, tiled=True)
    panel_tokens, panel_cotangent = gathered(tokens), gathered(cotangent)
    pre_part = jnp.dot(panel_tokens, up_weight, preferred_element_type=F32)
    back_part = lax.dot_general(
        panel_cotangent, down_weight, NT, preferred_element_type=F32
    )
    preact, back_grad = lax.psum((pre_part, back_part), "col")
    activated, factor = gelu_parts(preact)
    activated = activated.astype(BF16)
    delta = (back_grad * factor).astype(BF16)
    grad_down = lax.dot_general(
        activated, panel_cotangent, TN, preferred_element_type=F32
    )
    grad_up = lax.dot_general(panel_tokens, delta, TN, preferred_element_type=F32)
    grad_input = lax.psum_scatter(
        lax.dot_general(delta, up_weight, NT, preferred_element_type=F32),
        "row",
        scatter_dimension=0,
        tiled=True,
    )
    return (grad_input.astype(BF16), grad_up.astype(BF16), grad_down.astype(BF16))


def solution(mesh):
    row, col = mesh.shape["row"], mesh.shape["col"]

    def per_device(tokens, up_weight, down_weight, cotangent):
        args = (tokens, up_weight, down_weight, cotangent)
        short = row == 8 and tokens.shape[0] % 16 == 0
        if col == 2 and short:
            return split_plan(row, *args)
        return whole_plan(*args)

    in_specs = (
        P(("groups", "row"), "col"),
        P("col", "row"),
        P("row", "col"),
        P(("groups", "row"), "col"),
    )
    out_specs = (
        P(("groups", "row"), "col"),
        P(("groups", "col"), "row"),
        P(("groups", "row"), "col"),
    )
    return jax.shard_map(
        per_device, mesh=mesh, in_specs=in_specs, out_specs=out_specs, check_vma=False
    )
```
